32 devices in a mesh: parts: 2 (over y), row: 4 (over x, core), col: 4 (over z).
Axes of the slice: x: 2, y: 2, z: 4, core: 2. Of those that a mesh axis runs over, the one named last changes fastest.
Arguments:
- basis: float32 [2048, 16384], P(('parts', 'row'), 'col'), parts along dimension 0, may hold values from -6 to 6
- panel_one: float32 [32768, 256], P(('parts', 'col', 'row')), parts along dimension 0, may hold values from -192 to 192
- panel_two: float32 [32768, 256], P(('parts', 'col', 'row')), parts along dimension 0, may hold values from -192 to 192
- gradient: float32 [2048, 512], P(('parts', 'row')), parts along dimension 0, may hold values from -0.25 to 0.25
Outputs:
- new_basis: float32 [2048, 16384], P(('parts', 'row'), 'col'), parts along dimension 0
- rotated: float32 [1024, 16384], P(('parts', 'row'), 'col'), parts along dimension 0
The draws below stay inside these ranges and needn't reach their ends.
There are 2 independent parts, one for each index of `parts`. The reference program is written for one: setup_inputs(seed, part) draws one part's arguments, and reference() takes and returns one part's arrays. A program takes and returns all parts, laid end to end along the dimension named above; each array names one. Nothing has to cross between parts.
All inputs are finite; a program needn't handle non-finite values.
Results may differ from the reference program's by a relative error of at most 0.0001.
Values sent between devices are 32-bit elements; how exact they have to be, the bound alone decides.
A program may use at most 64 MiB of HBM per device.

```python
import math
import jax
import jax.numpy as jnp
from jax import lax

N = 16384
K = 256
GC = 512
ROWS = 1024


def make_panel(key, salt):
    key = jax.random.fold_in(key, salt)
    keys = jax.random.split(key, 4)
    noise = jnp.clip(jax.random.normal(keys[0], (N, K), jnp.float32), -4.0, 4.0)
    row_scale = jnp.exp(jax.random.uniform(keys[2], (N, 1), jnp.float32, 0.0, math.log(10.0)))
    shared = jnp.clip(jax.random.normal(keys[1], (N, 1), jnp.float32), -4.0, 4.0)
    col_scale = jnp.exp(jax.random.uniform(keys[3], (1, K), jnp.float32, 0.0, math.log(4.0)))
    return ((noise + 0.2 * shared) * row_scale * col_scale).astype(jnp.float32)


def draw_panel_one(key, part):
    return make_panel(key, 11)


def draw_panel_two(key, part):
    return make_panel(key, 23)


def spiked(array, stream_key, source, target, blocks, factor):
    owner, partner = [(jnp.arange(array.shape[position]) // (array.shape[position] // blocks)).reshape([-1 if axis == position else 1 for axis in range(array.ndim)]) for position in (source, target)]
    chosen = jax.random.permutation(stream_key, blocks)[partner]
    strong = (owner == chosen) | (owner == (partner + blocks // 2) % blocks)
    return jnp.where(strong, factor * array, array)


def levels(own_key, extent, cuts, low, largest):
    def one(axis_at, shards_of):
        heights = jax.random.uniform(jax.random.fold_in(jax.random.fold_in(own_key, 6), axis_at), (shards_of,), jnp.float32, low / len(cuts), largest / len(cuts))
        return jnp.repeat(jnp.exp(heights), extent[axis_at] // shards_of).reshape((-1,) + (1,) * (len(extent) - axis_at - 1))

    gain = one(*cuts[0])
    for cut in cuts[1:]:
        gain = gain * one(*cut)
    return gain


def normal_values(own_key, extent, scale, limit, cuts=(), kind=jnp.bfloat16):
    level = levels(own_key, extent, cuts, -0.22, 0.18) if cuts else 1.0
    drawn = jax.random.normal(own_key, extent, jnp.float32) * scale * level
    return jnp.minimum(jnp.maximum(drawn, -limit), limit).astype(kind)


def gaussian_with(key, shape, scale, reach, cuts, heavy, kind=jnp.bfloat16):
    entries = scale * jax.random.normal(key, shape, jnp.float32)
    if cuts:
        entries = entries * levels(key, shape, cuts, -0.22, 0.18)
    return jnp.clip(spiked(entries, jax.random.fold_in(key, 3), *heavy), -reach, reach).astype(kind)


def setup_inputs(seed: int = 0, part: int = 0) -> dict:
    splits = jax.random.split(jax.random.key(seed), 5)
    part_splits = jax.random.split(jax.random.fold_in(splits[4], part), 5)
    basis = normal_values(part_splits[0], (ROWS, N), 1.0, 6.0, ((0, 4), (1, 4)), jnp.float32)
    panel_one = draw_panel_one(jax.random.fold_in(jax.random.fold_in(splits[4], part), 71), part)
    panel_two = draw_panel_two(jax.random.fold_in(jax.random.fold_in(splits[4], part), 71), part)
    gradient = gaussian_with(part_splits[3], (ROWS, GC), ROWS ** -0.5, 0.25, ((0, 4),), (0, 1, 4, 2.0), jnp.float32)
    return dict(basis=basis, panel_one=panel_one, panel_two=panel_two, gradient=gradient)


def dot_high(left, right):
    return jnp.dot(left, right, precision=lax.Precision.HIGHEST, preferred_element_type=jnp.float32)


def tri_inverse(upper):
    size = upper.shape[0]
    width = 8
    count = size // width
    shaped = upper.reshape(count, width, count, width)
    selector = jnp.eye(count, dtype=upper.dtype)
    blocks = jnp.einsum("iajb,ij->iab", shaped, selector, precision=lax.Precision.HIGHEST)
    inverse = jnp.zeros_like(blocks)
    unit = jnp.eye(width, dtype=upper.dtype)
    for line in range(width - 1, -1, -1):
        known = jnp.einsum("bj,bjc->bc", blocks[:, line, :], inverse, precision=lax.Precision.HIGHEST)
        value = (unit[line][None, :] - known) / blocks[:, line, line][:, None]
        inverse = inverse.at[:, line, :].set(value)
    span = width
    while count > 1:
        shaped = upper.reshape(count, span, count, span)
        pairs = count // 2
        lefts = jnp.arange(pairs) * 2
        pick = ((jnp.arange(count)[None, :, None] == lefts[:, None, None]) & (jnp.arange(count)[None, None, :] == lefts[:, None, None] + 1)).astype(upper.dtype)
        corner = jnp.einsum("iajb,pij->pab", shaped, pick, precision=lax.Precision.HIGHEST)
        first = inverse[0::2]
        second = inverse[1::2]
        top = -jnp.einsum("pab,pbc->pac", jnp.einsum("pab,pbc->pac", first, corner, precision=lax.Precision.HIGHEST), second, precision=lax.Precision.HIGHEST)
        upper_half = jnp.concatenate([first, top], axis=2)
        lower_half = jnp.concatenate([jnp.zeros_like(second), second], axis=2)
        inverse = jnp.concatenate([upper_half, lower_half], axis=1)
        count = pairs
        span = span * 2
    return inverse[0]


def tri_factor(gram):
    upper = jnp.triu(gram, 1) + jnp.diag(jnp.diag(gram)) * 0.5
    return tri_inverse(upper)


def reference(basis, panel_one, panel_two, gradient):
    factor_one = tri_factor(dot_high(panel_one.T, panel_one))
    factor_two = tri_factor(dot_high(panel_two.T, panel_two))
    image_one = dot_high(basis, panel_one)
    middle = basis - dot_high(dot_high(image_one, factor_one), panel_one.T)
    image_two = dot_high(middle, panel_two)
    new_basis = middle - dot_high(dot_high(image_two, factor_two), panel_two.T)
    rotated = dot_high(gradient.T, new_basis)
    return new_basis, rotated
```

```python
import jax
import jax.numpy as jnp
from jax import lax
from jax.sharding import PartitionSpec as P

HIGH = lax.Precision.HIGH
HIGHEST = lax.Precision.HIGHEST


def dot(left, right, precision, dims=((1,), (0,))):
    return lax.dot_general(
        left, right, (dims, ((), ())), precision=precision, preferred_element_type=jnp.float32
    )


def tri_inverse(gram):
    size = gram.shape[0]
    rows = lax.broadcasted_iota(jnp.int32, (size, size), 0)
    cols = lax.broadcasted_iota(jnp.int32, (size, size), 1)
    inverse = jnp.where(rows == cols, 2.0 / jnp.where(rows == cols, gram, 1.0), 0.0)
    span = 1
    while span < size:
        pair = 2 * span
        corner = jnp.where(
            (rows // pair == cols // pair) & (rows // span < cols // span), gram, 0.0
        )
        inverse = inverse - dot(dot(inverse, corner, HIGHEST), inverse, HIGHEST)
        span = pair
    return inverse


def shards(basis, panel_one, panel_two, gradient):
    k = panel_one.shape[1]
    own = jnp.concatenate([panel_one, panel_two], axis=1)
    panel = lax.all_gather(own, "row", axis=0, tiled=True)
    gram = lax.psum(dot(own, own, HIGHEST, ((0,), (0,))), ("row", "col"))
    early = lax.psum_scatter(
        dot(gradient, basis, HIGH, ((0,), (0,))), "row", scatter_dimension=0, tiled=True
    )
    image = lax.psum(dot(basis, panel, HIGH), "col")
    factor_one = tri_inverse(gram[:k, :k])
    factor_two = tri_inverse(gram[k:, k:])
    one = dot(image[:, :k], factor_one, HIGHEST)
    two = dot(image[:, k:] - dot(one, gram[:k, k:], HIGHEST), factor_two, HIGHEST)
    weight = jnp.concatenate([one, two], axis=1)
    turned = lax.psum_scatter(
        dot(gradient, weight, HIGH, ((0,), (0,))), "row", scatter_dimension=0, tiled=True
    )
    new_basis = basis - dot(weight, panel, HIGH, ((1,), (1,)))
    rotated = early - dot(turned, panel, HIGH, ((1,), (1,)))
    return (new_basis, rotated)


def solution(mesh):
    return jax.shard_map(
        shards,
        mesh=mesh,
        in_specs=(
            P(("parts", "row"), "col"),
            P(("parts", "col", "row"), None),
            P(("parts", "col", "row"), None),
            P(("parts", "row"), None),
        ),
        out_specs=(P(("parts", "row"), "col"), P(("parts", "row"), "col")),
        check_vma=False,
    )
```

```python
import functools

import jax
import jax.numpy as jnp
from jax import lax
from jax.experimental import pallas as pl
from jax.experimental.pallas import tpu as pltpu
from jax.sharding import PartitionSpec as P

HIGHEST = lax.Precision.HIGHEST
MESH = pl.DeviceIdType.MESH
F32 = jnp.float32
BF16 = jnp.bfloat16


def dot_full(left, right):
    return jnp.dot(left, right, precision=HIGHEST, preferred_element_type=F32)


def split(value):
    high = value.astype(BF16)
    return high, (value - high.astype(F32)).astype(BF16)


def dot_split(left, right, across=0):
    def one(a, b):
        return lax.dot_general(a, b, (((1,), (across,)), ((), ())), preferred_element_type=F32)

    return one(left[0], right[0]) + (one(left[0], right[1]) + one(left[1], right[0]))


def remote(src, dst, send_sem, recv_sem, **device):
    return pltpu.make_async_remote_copy(
        src_ref=src,
        dst_ref=dst,
        send_sem=send_sem,
        recv_sem=recv_sem,
        device_id=device,
        device_id_type=MESH,
    )


def tri_inverse_pair(first, second):
    size = first.shape[0]
    rows = lax.broadcasted_iota(jnp.int32, (size, size), 0)
    cols = lax.broadcasted_iota(jnp.int32, (size, size), 1)
    eye = rows == cols

    def start(gram):
        return jnp.where(eye, 2.0 / jnp.where(eye, gram, 1.0), 0.0)

    def level(i, carry):
        half_rows = lax.shift_right_logical(rows, i)
        half_cols = lax.shift_right_logical(cols, i)
        pick = (half_cols == half_rows + 1) & ((half_rows & 1) == 0)

        def grow(inverse, gram):
            corner = jnp.where(pick, gram, 0.0)
            return inverse - dot_full(dot_full(inverse, corner), inverse)

        return grow(carry[0], first), grow(carry[1], second)

    return lax.fori_loop(0, size.bit_length() - 1, level, (start(first), start(second)))


def kernel(
    dims,
    basis, one, two, gradient,
    fresh, rotated,
    pg, ph, plo, bh, bl, gts, gtl, tsend, tkeep, trecv, xrecv,
    gm, g1, gz, g2, g3src, g3, gfull, yacc, y2, abuf, usend, urecv, ukeep, u2,
    pxs, pxr, pss, psr, g1sem, g2s, g2r, g3s, g3r, g4s, g4r, g5sem,
    ts, tr, xs, xr, ys, yr, as_, ar, u1sem, u2s, u2r,
):
    rows_n, cols_n, n, k, g, heads = dims
    big_r, big_c = cols_n // n, rows_n
    chips, depth = big_r // 2, big_c
    r, z = lax.axis_index("row"), lax.axis_index("col")
    c, x = lax.rem(r, 2), lax.div(r, 2)
    sib = r + 1 - 2 * c

    def chip(d):
        return lax.rem(x + d, chips) * 2 + c

    def chip_from(d):
        return lax.rem(x + chips - d, chips) * 2 + c

    def layer(d):
        return lax.rem(z + d, depth)

    def layer_from(d):
        return lax.rem(z + depth - d, depth)

    def strip(index, size):
        return pl.ds(pl.multiple_of(index * size, size), size)

    barrier = pltpu.get_barrier_semaphore()
    pl.semaphore_signal(barrier, inc=1, device_id={"row": sib}, device_id_type=MESH)
    for d in range(1, chips):
        pl.semaphore_signal(barrier, inc=1, device_id={"row": chip(d)}, device_id_type=MESH)
    for d in range(1, depth):
        pl.semaphore_signal(barrier, inc=1, device_id={"col": layer(d)}, device_id_type=MESH)
    pl.semaphore_wait(barrier, 1 + (chips - 1) + (depth - 1))

    panels = (one, two)
    nh = n // heads
    sends = []

    def go(copy):
        copy.start()
        sends.append(copy)

    def spot(owner, h, j):
        return pg.at[owner, pl.ds(h * nh, nh), pl.ds(j * k, k)]

    for h in range(heads):
        for j in range(2):
            q = 2 * h + j
            src = panels[j].at[pl.ds(h * nh, nh)]
            for d in range(1, chips):
                go(remote(src, spot(r, h, j), pxs.at[d - 1, q], pxr.at[d - 1, q], row=chip(d)))
            go(remote(src, spot(r, h, j), pss.at[0, q], psr.at[0, q], row=sib))

    one_t, two_t = one[...].T, two[...].T
    gm[0, :, :k] = dot_full(one_t, one[...])
    gm[0, :, k:] = dot_full(one_t, two[...])
    gm[1, :, :k] = dot_full(two_t, two[...])
    gm[1, :, k:] = jnp.zeros((k, k), F32)
    gram_one = remote(gm.at[1 - c], g1, g1sem.at[0], g1sem.at[1], row=sib)
    go(gram_one)

    for rr in range(big_r):
        bh[rr], bl[rr] = split(basis[:, rr * n:(rr + 1) * n])
    turned_g = gradient[...].T
    for rr in range(big_r):
        at = pl.ds((rr // 2) * g, g)
        gts[rr % 2, at], gtl[rr % 2, at] = split(turned_g[rr * g:(rr + 1) * g])
    for rr in range(big_r):
        tsend[rr] = dot_split((gts[1 - c], gtl[1 - c]), (bh[rr], bl[rr]))
        go(remote(tsend.at[rr], trecv.at[rr], ts.at[rr], tr.at[rr], row=sib))

    gram_one.wait_recv()
    gz[...] = gm[c] + g1[...]
    zs = k // depth
    for d in range(1, depth):
        go(remote(gz.at[strip(layer(d), zs)], g2.at[d - 1], g2s.at[d - 1], g2r.at[d - 1], col=layer(d)))

    for rr in range(big_r):
        tkeep[rr] = dot_split((gts[c], gtl[c]), (bh[rr], bl[rr]))

    def consume(owner, h, halves):
        at = pl.ds(h * nh, nh)
        for j in range(2):
            ph[owner, at, pl.ds(j * k, k)], plo[owner, at, pl.ds(j * k, k)] = split(halves[j])
        yacc[...] += dot_split(
            (bh[owner, :, at], bl[owner, :, at]), (ph[owner, at, :], plo[owner, at, :])
        )

    yacc[...] = jnp.zeros_like(yacc)
    for h in range(heads):
        at = pl.ds(h * nh, nh)
        consume(r, h, (one[at, :], two[at, :]))

    for d in range(1, depth):
        remote(g2.at[d - 1], g2.at[d - 1], g2s.at[d - 1], g2r.at[d - 1], col=layer(d)).wait_recv()
    total = gz[strip(z, zs), :]
    for d in range(1, depth):
        total = total + g2[d - 1]
    g3src[...] = total
    for d in range(1, chips):
        go(remote(g3src, g3.at[d - 1], g3s.at[d - 1], g3r.at[d - 1], row=chip(d)))

    def take_sibling(slot, owner, h):
        for j in range(2):
            q = 2 * h + j
            remote(spot(owner, h, j), spot(owner, h, j), pss.at[slot, q], psr.at[slot, q], row=sib).wait_recv()
        at = pl.ds(h * nh, nh)
        consume(owner, h, (pg[owner, at, :k], pg[owner, at, k:]))

    def take_chip(d, h):
        owner = chip_from(d)
        for j in range(2):
            q = 2 * h + j
            remote(spot(owner, h, j), spot(owner, h, j), pxs.at[d - 1, q], pxr.at[d - 1, q], row=chip(d)).wait_recv()
            go(remote(spot(owner, h, j), spot(owner, h, j), pss.at[d, q], psr.at[d, q], row=sib))
        at = pl.ds(h * nh, nh)
        consume(owner, h, (pg[owner, at, :k], pg[owner, at, k:]))

    def take_round(h):
        for d in range(1, chips):
            take_chip(d, h)
        for d in range(1, chips):
            take_sibling(d, chip_from(d) + 1 - 2 * c, h)

    for h in range(heads):
        take_sibling(0, sib, h)

    for d in range(1, chips):
        remote(g3.at[d - 1], g3.at[d - 1], g3s.at[d - 1], g3r.at[d - 1], row=chip(d)).wait_recv()
    total = g3src[...]
    for d in range(1, chips):
        total = total + g3[d - 1]
    gfull[c, strip(z, zs), :] = total
    mine = gfull.at[c, strip(z, zs)]
    for d in range(1, depth):
        go(remote(mine, mine, g4s.at[d - 1], g4r.at[d - 1], col=layer(d)))

    for rr in range(big_r):
        remote(trecv.at[rr], trecv.at[rr], ts.at[rr], tr.at[rr], row=sib).wait_recv()
        tkeep[rr] = tkeep[rr] + trecv[rr]

    early = heads // 2
    for h in range(early):
        take_round(h)

    for d in range(1, depth):
        theirs = gfull.at[c, strip(layer_from(d), zs)]
        remote(theirs, theirs, g4s.at[d - 1], g4r.at[d - 1], col=layer(d)).wait_recv()
    go(remote(gfull.at[c], gfull.at[c], g5sem.at[0], g5sem.at[1], row=sib))
    for h in range(early, heads - 1):
        take_round(h)
    other = gfull.at[1 - c]
    remote(other, other, g5sem.at[0], g5sem.at[1], row=sib).wait_recv()
    factor_one, factor_two = tri_inverse_pair(gfull[0, :, :k], gfull[1, :, :k])

    for rr in range(big_r):
        for d in range(1, chips):
            to = lax.rem(x + d, chips)
            go(remote(tkeep.at[rr, strip(to, g)], xrecv.at[d - 1, rr], xs.at[d - 1, rr], xr.at[d - 1, rr], row=chip(d)))
    take_round(heads - 1)

    rs = basis.shape[0] // depth
    for d in range(1, depth):
        go(remote(yacc.at[strip(layer(d), rs)], y2.at[d - 1], ys.at[d - 1], yr.at[d - 1], col=layer(d)))
    total = yacc[strip(z, rs), :]
    for d in range(1, depth):
        remote(y2.at[d - 1], y2.at[d - 1], ys.at[d - 1], yr.at[d - 1], col=layer(d)).wait_recv()
        total = total + y2[d - 1]
    weight_one = dot_full(total[:, :k], factor_one)
    weight_two = dot_full(total[:, k:] - dot_full(weight_one, gfull[0, :, k:]), factor_two)
    abuf[strip(z, rs), :k] = weight_one
    abuf[strip(z, rs), k:] = weight_two
    mine = abuf.at[strip(z, rs)]
    for d in range(1, depth):
        go(remote(mine, mine, as_.at[d - 1], ar.at[d - 1], col=layer(d)))
    for d in range(1, depth):
        theirs = abuf.at[strip(layer_from(d), rs)]
        remote(theirs, theirs, as_.at[d - 1], ar.at[d - 1], col=layer(d)).wait_recv()

    weight = split(abuf[...])
    usend[...] = dot_split((gts[1 - c], gtl[1 - c]), weight)
    turn = remote(usend, urecv, u1sem.at[0], u1sem.at[1], row=sib)
    go(turn)
    ukeep[...] = dot_split((gts[c], gtl[c]), weight)

    def update(rr):
        at = slice(rr * n, (rr + 1) * n)
        fresh[:, at] = basis[:, at] - dot_split(weight, (ph[rr], plo[rr]), 1)

    update(0)
    turn.wait_recv()
    ukeep[...] = ukeep[...] + urecv[...]
    for d in range(1, chips):
        to = lax.rem(x + d, chips)
        go(remote(ukeep.at[strip(to, g)], u2.at[d - 1], u2s.at[d - 1], u2r.at[d - 1], row=chip(d)))
    for rr in range(1, big_r):
        update(rr)
    turned = ukeep[strip(x, g), :]
    for d in range(1, chips):
        remote(u2.at[d - 1], u2.at[d - 1], u2s.at[d - 1], u2r.at[d - 1], row=chip(d)).wait_recv()
        turned = turned + u2[d - 1]
    turned = split(turned)
    for rr in range(big_r):
        value = tkeep[rr, strip(x, g), :] - dot_split(turned, (ph[rr], plo[rr]), 1)
        for d in range(1, chips):
            remote(xrecv.at[d - 1, rr], xrecv.at[d - 1, rr], xs.at[d - 1, rr], xr.at[d - 1, rr], row=chip(d)).wait_recv()
            value = value + xrecv[d - 1, rr]
        rotated[:, rr * n:(rr + 1) * n] = value
    for copy in sends:
        copy.wait_send()


def solution(mesh):
    big_r, depth = mesh.shape["row"], mesh.shape["col"]
    chips = big_r // 2

    def shards(basis, one, two, gradient):
        m, cols_n = basis.shape
        n, k = one.shape
        gc = gradient.shape[1]
        g = gc // big_r
        heads = 4 if n % 1024 == 0 else 1
        q = 2 * heads
        xo, zo = max(chips - 1, 1), max(depth - 1, 1)
        dma = pltpu.SemaphoreType.DMA
        vmem = pltpu.VMEM
        scratch = [
            vmem((big_r, n, 2 * k), F32),
            vmem((big_r, n, 2 * k), BF16),
            vmem((big_r, n, 2 * k), BF16),
            vmem((big_r, m, n), BF16),
            vmem((big_r, m, n), BF16),
            vmem((2, chips * g, m), BF16),
            vmem((2, chips * g, m), BF16),
            vmem((big_r, chips * g, n), F32),
            vmem((big_r, chips * g, n), F32),
            vmem((big_r, chips * g, n), F32),
            vmem((xo, big_r, g, n), F32),
            vmem((2, k, 2 * k), F32),
            vmem((k, 2 * k), F32),
            vmem((k, 2 * k), F32),
            vmem((zo, k // depth, 2 * k), F32),
            vmem((k // depth, 2 * k), F32),
            vmem((xo, k // depth, 2 * k), F32),
            vmem((2, k, 2 * k), F32),
            vmem((m, 2 * k), F32),
            vmem((zo, m // depth, 2 * k), F32),
            vmem((m, 2 * k), F32),
            vmem((chips * g, 2 * k), F32),
            vmem((chips * g, 2 * k), F32),
            vmem((chips * g, 2 * k), F32),
            vmem((xo, g, 2 * k), F32),
            dma((xo, q)), dma((xo, q)), dma((chips, q)), dma((chips, q)),
            dma((2,)), dma((zo,)), dma((zo,)), dma((xo,)), dma((xo,)),
            dma((zo,)), dma((zo,)), dma((2,)),
            dma((big_r,)), dma((big_r,)), dma((xo, big_r)), dma((xo, big_r)),
            dma((zo,)), dma((zo,)), dma((zo,)), dma((zo,)),
            dma((2,)), dma((xo,)), dma((xo,)),
        ]
        return pl.pallas_call(
            functools.partial(kernel, (depth, cols_n, n, k, g, heads)),
            out_shape=(
                jax.ShapeDtypeStruct((m, cols_n), F32),
                jax.ShapeDtypeStruct((g, cols_n), F32),
            ),
            in_specs=[pl.BlockSpec(memory_space=pltpu.VMEM)] * 4,
            out_specs=(pl.BlockSpec(memory_space=pltpu.VMEM),) * 2,
            scratch_shapes=scratch,
            compiler_params=pltpu.CompilerParams(
                collective_id=0, has_side_effects=True, vmem_limit_bytes=62 * 1024 * 1024
            ),
        )(basis, one, two, gradient)

    return jax.shard_map(
        shards,
        mesh=mesh,
        in_specs=(
            P(("parts", "row"), "col"),
            P(("parts", "col", "row"), None),
            P(("parts", "col", "row"), None),
            P(("parts", "row"), None),
        ),
        out_specs=(P(("parts", "row"), "col"), P(("parts", "row"), "col")),
        check_vma=False,
    )
```

```python
import functools

import jax
import jax.numpy as jnp
from jax import lax
from jax.experimental import pallas as pl
from jax.experimental.pallas import tpu as pltpu
from jax.sharding import PartitionSpec as P

HIGHEST = lax.Precision.HIGHEST
MESH = pl.DeviceIdType.MESH
F32 = jnp.float32
BF16 = jnp.bfloat16


def dot_full(left, right):
    return jnp.dot(left, right, precision=HIGHEST, preferred_element_type=F32)


def split(value):
    high = value.astype(BF16)
    return high, (value - high.astype(F32)).astype(BF16)


def dot_split(left, right, across=0):
    def one(a, b):
        return lax.dot_general(a, b, (((1,), (across,)), ((), ())), preferred_element_type=F32)

    return one(left[0], right[0]) + (one(left[0], right[1]) + one(left[1], right[0]))


def remote(src, dst, send_sem, recv_sem, **device):
    return pltpu.make_async_remote_copy(
        src_ref=src,
        dst_ref=dst,
        send_sem=send_sem,
        recv_sem=recv_sem,
        device_id=device,
        device_id_type=MESH,
    )


def tri_inverse_pair(first, second):
    size = first.shape[0]
    rows = lax.broadcasted_iota(jnp.int32, (size, size), 0)
    cols = lax.broadcasted_iota(jnp.int32, (size, size), 1)
    eye = rows == cols

    def start(gram):
        return jnp.where(eye, 2.0 / jnp.where(eye, gram, 1.0), 0.0)

    def level(i, carry):
        half_rows = lax.shift_right_logical(rows, i)
        half_cols = lax.shift_right_logical(cols, i)
        pick = (half_cols == half_rows + 1) & ((half_rows & 1) == 0)

        def grow(inverse, gram):
            corner = jnp.where(pick, gram, 0.0)
            return inverse - dot_full(dot_full(inverse, corner), inverse)

        return grow(carry[0], first), grow(carry[1], second)

    return lax.fori_loop(0, size.bit_length() - 1, level, (start(first), start(second)))


def kernel(
    dims,
    basis, one, two, gradient,
    fresh, rotated,
    pg, ph, plo, bh, bl, gts, gtl, tsend, tkeep, trecv, xrecv,
    gm, g1, gz, g2, g3src, g3, gfull, yacc, y2, abuf, usend, urecv, ukeep, u2,
    pxs, pxr, pss, psr, g1sem, g2s, g2r, g3s, g3r, g4s, g4r, g5sem,
    ts, tr, xs, xr, ys, yr, as_, ar, u1sem, u2s, u2r,
):
    rows_n, cols_n, n, k, g, heads = dims
    big_r, big_c = cols_n // n, rows_n
    chips, depth = big_r // 2, big_c
    r, z = lax.axis_index("row"), lax.axis_index("col")
    c, x = lax.rem(r, 2), lax.div(r, 2)
    sib = r + 1 - 2 * c

    def chip(d):
        return lax.rem(x + d, chips) * 2 + c

    def chip_from(d):
        return lax.rem(x + chips - d, chips) * 2 + c

    def layer(d):
        return lax.rem(z + d, depth)

    def layer_from(d):
        return lax.rem(z + depth - d, depth)

    def strip(index, size):
        return pl.ds(pl.multiple_of(index * size, size), size)

    barrier = pltpu.get_barrier_semaphore()
    pl.semaphore_signal(barrier, inc=1, device_id={"row": sib}, device_id_type=MESH)
    for d in range(1, chips):
        pl.semaphore_signal(barrier, inc=1, device_id={"row": chip(d)}, device_id_type=MESH)
    for d in range(1, depth):
        pl.semaphore_signal(barrier, inc=1, device_id={"col": layer(d)}, device_id_type=MESH)
    pl.semaphore_wait(barrier, 1 + (chips - 1) + (depth - 1))

    panels = (one, two)
    nh = n // heads
    sends = []

    def go(copy):
        copy.start()
        sends.append(copy)

    def spot(owner, h, j):
        return pg.at[owner, pl.ds(h * nh, nh), pl.ds(j * k, k)]

    def own(h, j):
        return panels[j].at[pl.ds(h * nh, nh)]

    def send_across(h):
        for j in range(2):
            q = 2 * h + j
            for d in range(1, chips):
                go(remote(own(h, j), spot(r, h, j), pxs.at[d - 1, q], pxr.at[d - 1, q], row=chip(d)))

    ahead = (heads + 1) // 2
    for h in range(ahead):
        send_across(h)

    one_t, two_t = one[...].T, two[...].T
    gm[0, :, :k] = dot_full(one_t, one[...])
    gm[0, :, k:] = dot_full(one_t, two[...])
    gm[1, :, :k] = dot_full(two_t, two[...])
    gm[1, :, k:] = jnp.zeros((k, k), F32)
    gram_one = remote(gm.at[1 - c], g1, g1sem.at[0], g1sem.at[1], row=sib)
    go(gram_one)

    for h in range(heads):
        for j in range(2):
            q = 2 * h + j
            go(remote(own(h, j), spot(r, h, j), pss.at[0, q], psr.at[0, q], row=sib))

    for rr in range(big_r):
        bh[rr], bl[rr] = split(basis[:, rr * n:(rr + 1) * n])
    turned_g = gradient[...].T
    for rr in range(big_r):
        at = pl.ds((rr // 2) * g, g)
        gts[rr % 2, at], gtl[rr % 2, at] = split(turned_g[rr * g:(rr + 1) * g])
    for rr in range(big_r):
        tsend[rr] = dot_split((gts[1 - c], gtl[1 - c]), (bh[rr], bl[rr]))
        go(remote(tsend.at[rr], trecv.at[rr], ts.at[rr], tr.at[rr], row=sib))

    gram_one.wait_recv()
    gz[...] = gm[c] + g1[...]
    zs = k // depth
    for d in range(1, depth):
        go(remote(gz.at[strip(layer(d), zs)], g2.at[d - 1], g2s.at[d - 1], g2r.at[d - 1], col=layer(d)))

    for rr in range(big_r):
        tkeep[rr] = dot_split((gts[c], gtl[c]), (bh[rr], bl[rr]))

    def consume(owner, h, halves):
        at = pl.ds(h * nh, nh)
        for j in range(2):
            ph[owner, at, pl.ds(j * k, k)], plo[owner, at, pl.ds(j * k, k)] = split(halves[j])
        yacc[...] += dot_split(
            (bh[owner, :, at], bl[owner, :, at]), (ph[owner, at, :], plo[owner, at, :])
        )

    yacc[...] = jnp.zeros_like(yacc)
    for h in range(heads):
        at = pl.ds(h * nh, nh)
        consume(r, h, (one[at, :], two[at, :]))

    for d in range(1, depth):
        remote(g2.at[d - 1], g2.at[d - 1], g2s.at[d - 1], g2r.at[d - 1], col=layer(d)).wait_recv()
    total = gz[strip(z, zs), :]
    for d in range(1, depth):
        total = total + g2[d - 1]
    g3src[...] = total
    for d in range(1, chips):
        go(remote(g3src, g3.at[d - 1], g3s.at[d - 1], g3r.at[d - 1], row=chip(d)))
    for h in range(ahead, heads):
        send_across(h)

    def take_sibling(slot, owner, h):
        for j in range(2):
            q = 2 * h + j
            remote(spot(owner, h, j), spot(owner, h, j), pss.at[slot, q], psr.at[slot, q], row=sib).wait_recv()
        at = pl.ds(h * nh, nh)
        consume(owner, h, (pg[owner, at, :k], pg[owner, at, k:]))

    def take_chip(d, h):
        owner = chip_from(d)
        for j in range(2):
            q = 2 * h + j
            remote(spot(owner, h, j), spot(owner, h, j), pxs.at[d - 1, q], pxr.at[d - 1, q], row=chip(d)).wait_recv()
            go(remote(spot(owner, h, j), spot(owner, h, j), pss.at[d, q], psr.at[d, q], row=sib))
        at = pl.ds(h * nh, nh)
        consume(owner, h, (pg[owner, at, :k], pg[owner, at, k:]))

    def take_round(h):
        for d in range(1, chips):
            take_chip(d, h)
        for d in range(1, chips):
            take_sibling(d, chip_from(d) + 1 - 2 * c, h)

    for h in range(heads):
        take_sibling(0, sib, h)

    for d in range(1, chips):
        remote(g3.at[d - 1], g3.at[d - 1], g3s.at[d - 1], g3r.at[d - 1], row=chip(d)).wait_recv()
    total = g3src[...]
    for d in range(1, chips):
        total = total + g3[d - 1]
    gfull[c, strip(z, zs), :] = total
    mine = gfull.at[c, strip(z, zs)]
    for d in range(1, depth):
        go(remote(mine, mine, g4s.at[d - 1], g4r.at[d - 1], col=layer(d)))

    for rr in range(big_r):
        remote(trecv.at[rr], trecv.at[rr], ts.at[rr], tr.at[rr], row=sib).wait_recv()
        tkeep[rr] = tkeep[rr] + trecv[rr]

    for h in range(heads - 1):
        take_round(h)

    for d in range(1, depth):
        theirs = gfull.at[c, strip(layer_from(d), zs)]
        remote(theirs, theirs, g4s.at[d - 1], g4r.at[d - 1], col=layer(d)).wait_recv()
    go(remote(gfull.at[c], gfull.at[c], g5sem.at[0], g5sem.at[1], row=sib))

    for rr in range(big_r):
        for d in range(1, chips):
            to = lax.rem(x + d, chips)
            go(remote(tkeep.at[rr, strip(to, g)], xrecv.at[d - 1, rr], xs.at[d - 1, rr], xr.at[d - 1, rr], row=chip(d)))
    take_round(heads - 1)

    rs = basis.shape[0] // depth
    for d in range(1, depth):
        go(remote(yacc.at[strip(layer(d), rs)], y2.at[d - 1], ys.at[d - 1], yr.at[d - 1], col=layer(d)))
    other = gfull.at[1 - c]
    remote(other, other, g5sem.at[0], g5sem.at[1], row=sib).wait_recv()
    factor_one, factor_two = tri_inverse_pair(gfull[0, :, :k], gfull[1, :, :k])
    total = yacc[strip(z, rs), :]
    for d in range(1, depth):
        remote(y2.at[d - 1], y2.at[d - 1], ys.at[d - 1], yr.at[d - 1], col=layer(d)).wait_recv()
        total = total + y2[d - 1]
    weight_one = dot_full(total[:, :k], factor_one)
    weight_two = dot_full(total[:, k:] - dot_full(weight_one, gfull[0, :, k:]), factor_two)
    abuf[strip(z, rs), :k] = weight_one
    abuf[strip(z, rs), k:] = weight_two
    mine = abuf.at[strip(z, rs)]
    for d in range(1, depth):
        go(remote(mine, mine, as_.at[d - 1], ar.at[d - 1], col=layer(d)))
    for d in range(1, depth):
        theirs = abuf.at[strip(layer_from(d), rs)]
        remote(theirs, theirs, as_.at[d - 1], ar.at[d - 1], col=layer(d)).wait_recv()

    weight = split(abuf[...])
    usend[...] = dot_split((gts[1 - c], gtl[1 - c]), weight)
    turn = remote(usend, urecv, u1sem.at[0], u1sem.at[1], row=sib)
    go(turn)
    ukeep[...] = dot_split((gts[c], gtl[c]), weight)

    def update(rr):
        at = slice(rr * n, (rr + 1) * n)
        fresh[:, at] = basis[:, at] - dot_split(weight, (ph[rr], plo[rr]), 1)

    update(0)
    turn.wait_recv()
    ukeep[...] = ukeep[...] + urecv[...]
    for d in range(1, chips):
        to = lax.rem(x + d, chips)
        go(remote(ukeep.at[strip(to, g)], u2.at[d - 1], u2s.at[d - 1], u2r.at[d - 1], row=chip(d)))
    for rr in range(1, big_r):
        update(rr)
    turned = ukeep[strip(x, g), :]
    for d in range(1, chips):
        remote(u2.at[d - 1], u2.at[d - 1], u2s.at[d - 1], u2r.at[d - 1], row=chip(d)).wait_recv()
        turned = turned + u2[d - 1]
    turned = split(turned)
    for rr in range(big_r):
        value = tkeep[rr, strip(x, g), :] - dot_split(turned, (ph[rr], plo[rr]), 1)
        for d in range(1, chips):
            remote(xrecv.at[d - 1, rr], xrecv.at[d - 1, rr], xs.at[d - 1, rr], xr.at[d - 1, rr], row=chip(d)).wait_recv()
            value = value + xrecv[d - 1, rr]
        rotated[:, rr * n:(rr + 1) * n] = value
    for copy in sends:
        copy.wait_send()


def solution(mesh):
    big_r, depth = mesh.shape["row"], mesh.shape["col"]
    chips = big_r // 2

    def shards(basis, one, two, gradient):
        m, cols_n = basis.shape
        n, k = one.shape
        gc = gradient.shape[1]
        g = gc // big_r
        heads = 4 if n % 1024 == 0 else 1
        q = 2 * heads
        xo, zo = max(chips - 1, 1), max(depth - 1, 1)
        dma = pltpu.SemaphoreType.DMA
        vmem = pltpu.VMEM
        scratch = [
            vmem((big_r, n, 2 * k), F32),
            vmem((big_r, n, 2 * k), BF16),
            vmem((big_r, n, 2 * k), BF16),
            vmem((big_r, m, n), BF16),
            vmem((big_r, m, n), BF16),
            vmem((2, chips * g, m), BF16),
            vmem((2, chips * g, m), BF16),
            vmem((big_r, chips * g, n), F32),
            vmem((big_r, chips * g, n), F32),
            vmem((big_r, chips * g, n), F32),
            vmem((xo, big_r, g, n), F32),
            vmem((2, k, 2 * k), F32),
            vmem((k, 2 * k), F32),
            vmem((k, 2 * k), F32),
            vmem((zo, k // depth, 2 * k), F32),
            vmem((k // depth, 2 * k), F32),
            vmem((xo, k // depth, 2 * k), F32),
            vmem((2, k, 2 * k), F32),
            vmem((m, 2 * k), F32),
            vmem((zo, m // depth, 2 * k), F32),
            vmem((m, 2 * k), F32),
            vmem((chips * g, 2 * k), F32),
            vmem((chips * g, 2 * k), F32),
            vmem((chips * g, 2 * k), F32),
            vmem((xo, g, 2 * k), F32),
            dma((xo, q)), dma((xo, q)), dma((chips, q)), dma((chips, q)),
            dma((2,)), dma((zo,)), dma((zo,)), dma((xo,)), dma((xo,)),
            dma((zo,)), dma((zo,)), dma((2,)),
            dma((big_r,)), dma((big_r,)), dma((xo, big_r)), dma((xo, big_r)),
            dma((zo,)), dma((zo,)), dma((zo,)), dma((zo,)),
            dma((2,)), dma((xo,)), dma((xo,)),
        ]
        return pl.pallas_call(
            functools.partial(kernel, (depth, cols_n, n, k, g, heads)),
            out_shape=(
                jax.ShapeDtypeStruct((m, cols_n), F32),
                jax.ShapeDtypeStruct((g, cols_n), F32),
            ),
            in_specs=[pl.BlockSpec(memory_space=pltpu.VMEM)] * 4,
            out_specs=(pl.BlockSpec(memory_space=pltpu.VMEM),) * 2,
            scratch_shapes=scratch,
            compiler_params=pltpu.CompilerParams(
                collective_id=0, has_side_effects=True, vmem_limit_bytes=62 * 1024 * 1024
            ),
        )(basis, one, two, gradient)

    return jax.shard_map(
        shards,
        mesh=mesh,
        in_specs=(
            P(("parts", "row"), "col"),
            P(("parts", "col", "row"), None),
            P(("parts", "col", "row"), None),
            P(("parts", "row"), None),
        ),
        out_specs=(P(("parts", "row"), "col"), P(("parts", "row"), "col")),
        check_vma=False,
    )
```

```python
import functools

import jax
import jax.numpy as jnp
from jax import lax
from jax.experimental import pallas as pl
from jax.experimental.pallas import tpu as pltpu
from jax.sharding import PartitionSpec as P

HIGHEST = lax.Precision.HIGHEST
MESH = pl.DeviceIdType.MESH
F32 = jnp.float32
BF16 = jnp.bfloat16


def dot_full(left, right):
    return jnp.dot(left, right, precision=HIGHEST, preferred_element_type=F32)


def split(value):
    high = value.astype(BF16)
    return high, (value - high.astype(F32)).astype(BF16)


def dot_split(left, right, across=0):
    def one(a, b):
        return lax.dot_general(a, b, (((1,), (across,)), ((), ())), preferred_element_type=F32)

    return one(left[0], right[0]) + (one(left[0], right[1]) + one(left[1], right[0]))


def remote(src, dst, send_sem, recv_sem, **device):
    return pltpu.make_async_remote_copy(
        src_ref=src,
        dst_ref=dst,
        send_sem=send_sem,
        recv_sem=recv_sem,
        device_id=device,
        device_id_type=MESH,
    )


def tri_inverse_pair(first, second):
    size = first.shape[0]
    rows = lax.broadcasted_iota(jnp.int32, (size, size), 0)
    cols = lax.broadcasted_iota(jnp.int32, (size, size), 1)
    eye = rows == cols

    def start(gram):
        return jnp.where(eye, 2.0 / jnp.where(eye, gram, 1.0), 0.0)

    def level(i, carry):
        half_rows = lax.shift_right_logical(rows, i)
        half_cols = lax.shift_right_logical(cols, i)
        pick = (half_cols == half_rows + 1) & ((half_rows & 1) == 0)

        def grow(inverse, gram):
            corner = jnp.where(pick, gram, 0.0)
            return inverse - dot_full(dot_full(inverse, corner), inverse)

        return grow(carry[0], first), grow(carry[1], second)

    return lax.fori_loop(0, size.bit_length() - 1, level, (start(first), start(second)))


def kernel(
    dims,
    basis, one, two, gradient,
    fresh, rotated,
    pg, ph, plo, bh, bl, gts, gtl, tsend, tkeep, trecv, xrecv,
    gm, g1, gz, g2, g3src, g3, gfull, yacc, y2, abuf, usend, urecv, ukeep, u2,
    pxs, pxr, pss, psr, g1sem, g2s, g2r, g3s, g3r, g4s, g4r, g5sem,
    ts, tr, xs, xr, ys, yr, as_, ar, u1sem, u2s, u2r,
):
    rows_n, cols_n, n, k, g, heads = dims
    big_r, big_c = cols_n // n, rows_n
    chips, depth = big_r // 2, big_c
    r, z = lax.axis_index("row"), lax.axis_index("col")
    c, x = lax.rem(r, 2), lax.div(r, 2)
    sib = r + 1 - 2 * c

    def chip(d):
        return lax.rem(x + d, chips) * 2 + c

    def chip_from(d):
        return lax.rem(x + chips - d, chips) * 2 + c

    def layer(d):
        return lax.rem(z + d, depth)

    def layer_from(d):
        return lax.rem(z + depth - d, depth)

    def strip(index, size):
        return pl.ds(pl.multiple_of(index * size, size), size)

    barrier = pltpu.get_barrier_semaphore()
    pl.semaphore_signal(barrier, inc=1, device_id={"row": sib}, device_id_type=MESH)
    for d in range(1, chips):
        pl.semaphore_signal(barrier, inc=1, device_id={"row": chip(d)}, device_id_type=MESH)
    for d in range(1, depth):
        pl.semaphore_signal(barrier, inc=1, device_id={"col": layer(d)}, device_id_type=MESH)
    pl.semaphore_wait(barrier, 1 + (chips - 1) + (depth - 1))

    panels = (one, two)
    nh = n // heads
    sends = []

    def go(copy):
        copy.start()
        sends.append(copy)

    def spot(owner, h, j):
        return pg.at[owner, pl.ds(h * nh, nh), pl.ds(j * k, k)]

    def own(h, j):
        return panels[j].at[pl.ds(h * nh, nh)]

    order = [(j, h) for j in range(2) for h in range(heads)]

    def send_across(j, h):
        q = 2 * h + j
        for d in range(1, chips):
            go(remote(own(h, j), spot(r, h, j), pxs.at[d - 1, q], pxr.at[d - 1, q], row=chip(d)))

    for j, h in order[:heads]:
        send_across(j, h)

    one_t, two_t = one[...].T, two[...].T
    gm[0, :, :k] = dot_full(one_t, one[...])
    gm[0, :, k:] = dot_full(one_t, two[...])
    gm[1, :, :k] = dot_full(two_t, two[...])
    gm[1, :, k:] = jnp.zeros((k, k), F32)
    gram_one = remote(gm.at[1 - c], g1, g1sem.at[0], g1sem.at[1], row=sib)
    go(gram_one)

    for j, h in order:
        q = 2 * h + j
        go(remote(own(h, j), spot(r, h, j), pss.at[0, q], psr.at[0, q], row=sib))

    for rr in range(big_r):
        bh[rr], bl[rr] = split(basis[:, rr * n:(rr + 1) * n])
    turned_g = gradient[...].T
    for rr in range(big_r):
        at = pl.ds((rr // 2) * g, g)
        gts[rr % 2, at], gtl[rr % 2, at] = split(turned_g[rr * g:(rr + 1) * g])
    for rr in range(big_r):
        tsend[rr] = dot_split((gts[1 - c], gtl[1 - c]), (bh[rr], bl[rr]))
        go(remote(tsend.at[rr], trecv.at[rr], ts.at[rr], tr.at[rr], row=sib))

    gram_one.wait_recv()
    gz[...] = gm[c] + g1[...]
    zs = k // depth
    for d in range(1, depth):
        go(remote(gz.at[strip(layer(d), zs)], g2.at[d - 1], g2s.at[d - 1], g2r.at[d - 1], col=layer(d)))

    for rr in range(big_r):
        tkeep[rr] = dot_split((gts[c], gtl[c]), (bh[rr], bl[rr]))

    def consume(owner, j, h, half):
        at, side = pl.ds(h * nh, nh), pl.ds(j * k, k)
        high, low = split(half)
        ph[owner, at, side], plo[owner, at, side] = high, low
        yacc[:, side] += dot_split((bh[owner, :, at], bl[owner, :, at]), (high, low))

    yacc[...] = jnp.zeros_like(yacc)
    for j, h in order:
        consume(r, j, h, own(h, j)[...])

    for d in range(1, depth):
        remote(g2.at[d - 1], g2.at[d - 1], g2s.at[d - 1], g2r.at[d - 1], col=layer(d)).wait_recv()
    total = gz[strip(z, zs), :]
    for d in range(1, depth):
        total = total + g2[d - 1]
    g3src[...] = total
    for d in range(1, chips):
        go(remote(g3src, g3.at[d - 1], g3s.at[d - 1], g3r.at[d - 1], row=chip(d)))
    for j, h in order[heads:]:
        send_across(j, h)

    def take_sibling(slot, owner, j, h):
        q = 2 * h + j
        here = spot(owner, h, j)
        remote(here, here, pss.at[slot, q], psr.at[slot, q], row=sib).wait_recv()
        consume(owner, j, h, here[...])

    def take_chip(d, j, h):
        q = 2 * h + j
        owner = chip_from(d)
        here = spot(owner, h, j)
        remote(here, here, pxs.at[d - 1, q], pxr.at[d - 1, q], row=chip(d)).wait_recv()
        go(remote(here, here, pss.at[d, q], psr.at[d, q], row=sib))
        consume(owner, j, h, here[...])

    def take_round(j, h):
        for d in range(1, chips):
            take_chip(d, j, h)
        for d in range(1, chips):
            take_sibling(d, chip_from(d) + 1 - 2 * c, j, h)

    for j, h in order:
        take_sibling(0, sib, j, h)

    for d in range(1, chips):
        remote(g3.at[d - 1], g3.at[d - 1], g3s.at[d - 1], g3r.at[d - 1], row=chip(d)).wait_recv()
    total = g3src[...]
    for d in range(1, chips):
        total = total + g3[d - 1]
    gfull[c, strip(z, zs), :] = total
    mine = gfull.at[c, strip(z, zs)]
    for d in range(1, depth):
        go(remote(mine, mine, g4s.at[d - 1], g4r.at[d - 1], col=layer(d)))

    for rr in range(big_r):
        remote(trecv.at[rr], trecv.at[rr], ts.at[rr], tr.at[rr], row=sib).wait_recv()
        tkeep[rr] = tkeep[rr] + trecv[rr]

    rs = basis.shape[0] // depth
    sides = (pl.ds(0, k), pl.ds(k, k))

    def image_out(j):
        for d in range(1, depth):
            go(remote(
                yacc.at[strip(layer(d), rs), sides[j]], y2.at[d - 1, :, sides[j]],
                ys.at[j, d - 1], yr.at[j, d - 1], col=layer(d),
            ))

    def image_in(j):
        total = yacc[strip(z, rs), sides[j]]
        for d in range(1, depth):
            here = y2.at[d - 1, :, sides[j]]
            remote(here, here, ys.at[j, d - 1], yr.at[j, d - 1], col=layer(d)).wait_recv()
            total = total + here[...]
        return total

    def weight_out(j, value):
        abuf[strip(z, rs), sides[j]] = value
        mine = abuf.at[strip(z, rs), sides[j]]
        for d in range(1, depth):
            go(remote(mine, mine, as_.at[j, d - 1], ar.at[j, d - 1], col=layer(d)))

    for j, h in order[:heads]:
        take_round(j, h)
    image_out(0)
    for j, h in order[heads:-1]:
        take_round(j, h)

    for d in range(1, depth):
        theirs = gfull.at[c, strip(layer_from(d), zs)]
        remote(theirs, theirs, g4s.at[d - 1], g4r.at[d - 1], col=layer(d)).wait_recv()
    go(remote(gfull.at[c], gfull.at[c], g5sem.at[0], g5sem.at[1], row=sib))

    for rr in range(big_r):
        for d in range(1, chips):
            to = lax.rem(x + d, chips)
            go(remote(tkeep.at[rr, strip(to, g)], xrecv.at[d - 1, rr], xs.at[d - 1, rr], xr.at[d - 1, rr], row=chip(d)))
    other = gfull.at[1 - c]
    remote(other, other, g5sem.at[0], g5sem.at[1], row=sib).wait_recv()
    factor_one, factor_two = tri_inverse_pair(gfull[0, :, :k], gfull[1, :, :k])
    weight_one = dot_full(image_in(0), factor_one)
    weight_out(0, weight_one)
    cross = dot_full(weight_one, gfull[0, :, k:])
    take_round(*order[-1])
    image_out(1)
    weight_out(1, dot_full(image_in(1) - cross, factor_two))
    for j in range(2):
        for d in range(1, depth):
            theirs = abuf.at[strip(layer_from(d), rs), sides[j]]
            remote(theirs, theirs, as_.at[j, d - 1], ar.at[j, d - 1], col=layer(d)).wait_recv()

    weight = split(abuf[...])
    usend[...] = dot_split((gts[1 - c], gtl[1 - c]), weight)
    turn = remote(usend, urecv, u1sem.at[0], u1sem.at[1], row=sib)
    go(turn)
    ukeep[...] = dot_split((gts[c], gtl[c]), weight)

    def update(rr):
        at = slice(rr * n, (rr + 1) * n)
        fresh[:, at] = basis[:, at] - dot_split(weight, (ph[rr], plo[rr]), 1)

    update(0)
    turn.wait_recv()
    ukeep[...] = ukeep[...] + urecv[...]
    for d in range(1, chips):
        to = lax.rem(x + d, chips)
        go(remote(ukeep.at[strip(to, g)], u2.at[d - 1], u2s.at[d - 1], u2r.at[d - 1], row=chip(d)))
    for rr in range(1, big_r):
        update(rr)
    turned = ukeep[strip(x, g), :]
    for d in range(1, chips):
        remote(u2.at[d - 1], u2.at[d - 1], u2s.at[d - 1], u2r.at[d - 1], row=chip(d)).wait_recv()
        turned = turned + u2[d - 1]
    turned = split(turned)
    for rr in range(big_r):
        value = tkeep[rr, strip(x, g), :] - dot_split(turned, (ph[rr], plo[rr]), 1)
        for d in range(1, chips):
            remote(xrecv.at[d - 1, rr], xrecv.at[d - 1, rr], xs.at[d - 1, rr], xr.at[d - 1, rr], row=chip(d)).wait_recv()
            value = value + xrecv[d - 1, rr]
        rotated[:, rr * n:(rr + 1) * n] = value
    for copy in sends:
        copy.wait_send()


def solution(mesh):
    big_r, depth = mesh.shape["row"], mesh.shape["col"]
    chips = big_r // 2

    def shards(basis, one, two, gradient):
        m, cols_n = basis.shape
        n, k = one.shape
        gc = gradient.shape[1]
        g = gc // big_r
        heads = 4 if n % 1024 == 0 else 1
        q = 2 * heads
        xo, zo = max(chips - 1, 1), max(depth - 1, 1)
        dma = pltpu.SemaphoreType.DMA
        vmem = pltpu.VMEM
        scratch = [
            vmem((big_r, n, 2 * k), F32),
            vmem((big_r, n, 2 * k), BF16),
            vmem((big_r, n, 2 * k), BF16),
            vmem((big_r, m, n), BF16),
            vmem((big_r, m, n), BF16),
            vmem((2, chips * g, m), BF16),
            vmem((2, chips * g, m), BF16),
            vmem((big_r, chips * g, n), F32),
            vmem((big_r, chips * g, n), F32),
            vmem((big_r, chips * g, n), F32),
            vmem((xo, big_r, g, n), F32),
            vmem((2, k, 2 * k), F32),
            vmem((k, 2 * k), F32),
            vmem((k, 2 * k), F32),
            vmem((zo, k // depth, 2 * k), F32),
            vmem((k // depth, 2 * k), F32),
            vmem((xo, k // depth, 2 * k), F32),
            vmem((2, k, 2 * k), F32),
            vmem((m, 2 * k), F32),
            vmem((zo, m // depth, 2 * k), F32),
            vmem((m, 2 * k), F32),
            vmem((chips * g, 2 * k), F32),
            vmem((chips * g, 2 * k), F32),
            vmem((chips * g, 2 * k), F32),
            vmem((xo, g, 2 * k), F32),
            dma((xo, q)), dma((xo, q)), dma((chips, q)), dma((chips, q)),
            dma((2,)), dma((zo,)), dma((zo,)), dma((xo,)), dma((xo,)),
            dma((zo,)), dma((zo,)), dma((2,)),
            dma((big_r,)), dma((big_r,)), dma((xo, big_r)), dma((xo, big_r)),
            dma((2, zo)), dma((2, zo)), dma((2, zo)), dma((2, zo)),
            dma((2,)), dma((xo,)), dma((xo,)),
        ]
        return pl.pallas_call(
            functools.partial(kernel, (depth, cols_n, n, k, g, heads)),
            out_shape=(
                jax.ShapeDtypeStruct((m, cols_n), F32),
                jax.ShapeDtypeStruct((g, cols_n), F32),
            ),
            in_specs=[pl.BlockSpec(memory_space=pltpu.VMEM)] * 4,
            out_specs=(pl.BlockSpec(memory_space=pltpu.VMEM),) * 2,
            scratch_shapes=scratch,
            compiler_params=pltpu.CompilerParams(
                collective_id=0, has_side_effects=True, vmem_limit_bytes=62 * 1024 * 1024
            ),
        )(basis, one, two, gradient)

    return jax.shard_map(
        shards,
        mesh=mesh,
        in_specs=(
            P(("parts", "row"), "col"),
            P(("parts", "col", "row"), None),
            P(("parts", "col", "row"), None),
            P(("parts", "row"), None),
        ),
        out_specs=(P(("parts", "row"), "col"), P(("parts", "row"), "col")),
        check_vma=False,
    )
```
